256 devices in a mesh: blk: 64 (over y, z, core), sub: 4 (over x).
Axes of the slice: x: 4, y: 4, z: 8, core: 2. Of those that a mesh axis runs over, the one named last changes fastest.
Arguments:
- residual_rhs: float32 [6, 196608], P(None, ('blk', 'sub')), may hold values from -6 to 6
- diag_blocks: bfloat16 [6, 6, 196608], P(None, None, ('blk', 'sub')), may hold values from -1.5 to 6, as said below
- jacobian_blocks: bfloat16 [6, 6, 6, 196608], P(None, None, None, ('blk', 'sub')), may hold values from -1.5 to 1.5
- neighbors: int32 [6, 196608], P(None, ('blk', 'sub')), may hold values from 0 to 1535, as said below
- partner: int32 [64], replicated, may hold values from 0 to 63, as said below
- fringe_source: int32 [131072], P(('blk', 'sub')), may hold values from 0 to 767
- fringe_weight: float32 [131072], P(('blk', 'sub')), may hold values from 0.5 to 2
- fringe_donor: int32 [131072], P(('blk', 'sub')), may hold values from 0 to 511
- metric_sens: bfloat16 [3, 6, 196608], P(None, None, ('blk', 'sub')), may hold values from -6 to 6
- warp_row: int32 [524288], P(('blk', 'sub')), may hold values from 0 to 767
- warp_node: int32 [524288], P(('blk', 'sub')), may hold values from 0 to 8191
- warp_weight: float32 [524288], P(('blk', 'sub')), may hold values from 0.05 to 0.3
Outputs:
- adjoint_state: float32 [6, 196608], P(None, ('blk', 'sub'))
- surface_sens: float32 [3, 8192], P(None, 'blk')
The draws below stay inside these ranges and needn't reach their ends.
Inputs may be any that keep to these rules, and one draw needn't show every extreme that they name: `neighbors`: indices into the window: below 256 the lower rim, then 768 own rows, then 256 upper rim, then 256 partner rows. partner[partner[b]] = b and partner[b] != b. `diag_blocks`: each block's diagonal entries are 2.5 or more.
All inputs are finite; a program needn't handle non-finite values.
Results may differ from the reference program's by a relative error of at most 0.0003.
Values sent between devices are 32-bit elements; how exact they have to be, the bound alone decides.
A program may use at most 128 MiB of HBM per device.

```python
import math
import jax
import jax.numpy as jnp
import numpy as np
from jax import lax

FIELDS = 6
NEIGH = 6
SWEEPS = 3
CELLS_DEV = 512
MIGR_DEV = 256
RIM = 256
CAP = 8
WARP_DEV = 2048
ROWS = 768
NODES = 8192
N_BLK = 64
N_SUB = 4


def draw_neighbors(key, part):
    key = jax.random.fold_in(key, 11)
    keys = jax.random.split(key, 4)
    total = N_BLK * N_SUB * ROWS
    region = jax.random.randint(keys[0], (NEIGH, total), 0, 16)
    spot = jax.random.randint(keys[1], (NEIGH, total), 0, ROWS)
    rim_spot = jax.random.randint(keys[2], (NEIGH, total), 0, RIM)
    mate_spot = jax.random.randint(keys[3], (NEIGH, total), 0, MIGR_DEV)
    own = RIM + spot
    upper = RIM + ROWS + rim_spot
    mates = 2 * RIM + ROWS + mate_spot
    chosen = jnp.where(region == 0, rim_spot, jnp.where(region == 1, upper, jnp.where(region == 2, mates, own)))
    return chosen.astype(jnp.int32)


def draw_partner(key, part):
    key = jax.random.fold_in(key, 23)
    key_pick, key_order = jax.random.split(key)
    half = N_BLK // 2
    first = jax.random.randint(key_pick, (), 0, half).astype(jnp.int32)
    second = first + half
    order = jax.random.permutation(key_order, N_BLK).astype(jnp.int32)
    places = jnp.arange(N_BLK, dtype=jnp.int32) + 2
    scores = jnp.where(order == first, 0, jnp.where(order == second, 1, places))
    arranged = order[jnp.argsort(scores, stable=True)]
    evens = arranged[0::2]
    odds = arranged[1::2]
    mapping = jnp.zeros((N_BLK,), jnp.int32).at[evens].set(odds).at[odds].set(evens)
    return mapping


def draw_diag_blocks(key, part):
    key = jax.random.fold_in(key, 37)
    key_off, key_piv = jax.random.split(key)
    total = N_BLK * N_SUB * ROWS
    shape = (FIELDS, FIELDS, total)
    offdiag = jnp.clip(0.3 * jax.random.normal(key_off, shape, jnp.float32), -1.5, 1.5)
    pivot = jax.random.uniform(key_piv, shape, jnp.float32, 2.5, 4.0)
    rows_i = lax.broadcasted_iota(jnp.int32, shape, 0)
    cols_i = lax.broadcasted_iota(jnp.int32, shape, 1)
    return jnp.where(rows_i == cols_i, pivot, offdiag).astype(jnp.bfloat16)


def place_ends(values, own_key, smallest, high):
    extent = values.shape
    spot = [jax.random.randint(jax.random.fold_in(own_key, axis), (), 0, extent[axis]) for axis in range(len(extent))]
    values = values.at[tuple(spot)].set(smallest)
    longest = extent.index(max(extent))
    spot[longest] = (spot[longest] + 1) % extent[longest]
    return values.at[tuple(spot)].set(high)


def levels(rng, extent, pieces, smallest, high):
    loudness, own = 1.0, jax.random.fold_in(rng, 6)
    for position, parts in pieces:
        steps = jnp.exp(jax.random.uniform(jax.random.fold_in(own, position), (parts,), jnp.float32, smallest / len(pieces), high / len(pieces)))
        loudness = loudness * jnp.repeat(steps, extent[position] // parts).reshape([-1 if axis == position else 1 for axis in range(len(extent))])
    return loudness


def rank_table(number_of, lean):
    weights = [(1 << 20) // math.isqrt(rank ** lean) + 1 for rank in range(1, number_of + 1)]
    width = 1 + sum(weights) // (1 << 30)
    return np.cumsum(np.array([max(1, weight // width) for weight in weights]))


def skewed_ids(key, extent, amount, slope):
    grid = rank_table(amount, slope)
    lot = jax.random.randint(jax.random.fold_in(key, 1), extent, 0, int(grid[amount - 1]))
    rank = jnp.searchsorted(jnp.asarray(grid, jnp.int32), lot, side="right")
    return jax.random.permutation(jax.random.fold_in(key, 2), amount)[rank].astype(jnp.int32)


def normal_values(stream_key, shape, deviation, reach, pieces=(), kind=jnp.bfloat16):
    array = deviation * jax.random.normal(stream_key, shape, jnp.float32)
    if pieces:
        array = array * levels(stream_key, shape, pieces, -0.22, 0.18)
    return jnp.clip(array, -reach, reach).astype(kind)


def setup_inputs(seed: int = 0) -> dict:
    key_of = jax.random.split(jax.random.key(seed), 13)
    return {
        "residual_rhs": normal_values(key_of[0], (FIELDS, N_BLK * N_SUB * ROWS), 1.0, 6.0, ((1, 256),), jnp.float32),
        "diag_blocks": draw_diag_blocks(jax.random.fold_in(key_of[12], 71), 0),
        "jacobian_blocks": normal_values(key_of[2], (NEIGH, FIELDS, FIELDS, N_BLK * N_SUB * ROWS), 0.3, 1.5, ((3, 256),)),
        "neighbors": draw_neighbors(jax.random.fold_in(key_of[12], 71), 0),
        "partner": draw_partner(jax.random.fold_in(key_of[12], 71), 0),
        "fringe_source": place_ends(jax.random.randint(key_of[5], (N_BLK * N_SUB * N_BLK * CAP,), 0, ROWS), jax.random.fold_in(key_of[5], 1), 0, ROWS - 1).astype(jnp.int32),
        "fringe_weight": jnp.clip(jnp.exp(math.log(2.0) - 1.3862944 * jax.random.uniform(key_of[6], (N_BLK * N_SUB * N_BLK * CAP,), jnp.float32) ** levels(key_of[6], (N_BLK * N_SUB * N_BLK * CAP,), ((0, 256),), -0.2, 0.2)), 0.5, 2.0),
        "fringe_donor": place_ends(jax.random.randint(key_of[7], (N_BLK * N_SUB * N_BLK * CAP,), 0, CELLS_DEV), jax.random.fold_in(key_of[7], 1), 0, CELLS_DEV - 1).astype(jnp.int32),
        "metric_sens": normal_values(key_of[8], (3, FIELDS, N_BLK * N_SUB * ROWS), 1.0, 6.0, ((2, 256),)),
        "warp_row": place_ends(jax.random.randint(key_of[9], (N_BLK * N_SUB * WARP_DEV,), 0, ROWS), jax.random.fold_in(key_of[9], 1), 0, ROWS - 1).astype(jnp.int32),
        "warp_node": place_ends(skewed_ids(key_of[10], (N_BLK * N_SUB * WARP_DEV,), NODES, 1), jax.random.fold_in(key_of[10], 3), 0, NODES - 1).astype(jnp.int32),
        "warp_weight": jnp.clip(jnp.exp(math.log(0.3) - 1.7917595 * jax.random.uniform(key_of[11], (N_BLK * N_SUB * WARP_DEV,), jnp.float32) ** levels(key_of[11], (N_BLK * N_SUB * WARP_DEV,), ((0, 256),), -0.2, 0.2)), 0.05, 0.3),
    }


relaxation = 0.8


def apply_operator(state, diag_blocks, jacobian_blocks, neighbors, partner, fringe_source, fringe_weight, fringe_donor):
    devices = N_BLK * N_SUB
    shaped = state.reshape(FIELDS, devices, ROWS)
    blank = jnp.zeros((FIELDS, 1, RIM), jnp.float32)
    lower = jnp.concatenate([blank, shaped[:, :-1, CELLS_DEV - RIM:CELLS_DEV]], axis=1)
    upper = jnp.concatenate([shaped[:, 1:, :RIM], blank], axis=1)
    device_ids = jnp.arange(devices, dtype=jnp.int32)
    group_ids = device_ids // N_SUB
    mate_ids = partner[group_ids] * N_SUB + device_ids % N_SUB
    mates = shaped[:, mate_ids, CELLS_DEV:]
    window = jnp.concatenate([lower, shaped, upper, mates], axis=2)
    span = window.shape[2]
    flat_window = window.reshape(FIELDS, devices * span)
    offsets = jnp.repeat(device_ids * span, ROWS)
    image = jnp.zeros((FIELDS, devices * ROWS), jnp.float32)
    for f in range(FIELDS):
        image = image + diag_blocks[f].astype(jnp.float32) * state[f][None, :]
    for k in range(NEIGH):
        picked = flat_window[:, neighbors[k] + offsets]
        for f in range(FIELDS):
            image = image + jacobian_blocks[k, f].astype(jnp.float32) * picked[f][None, :]
    sources = fringe_source.reshape(devices, N_BLK, CAP)
    donors = fringe_donor.reshape(devices, N_BLK, CAP)
    target_dev = jnp.arange(N_BLK, dtype=jnp.int32)[None, :, None] * N_SUB + (device_ids % N_SUB)[:, None, None]
    target_dev = jnp.broadcast_to(target_dev, (devices, N_BLK, CAP))
    sender_group = jnp.broadcast_to(group_ids[:, None, None], (devices, N_BLK, CAP))
    slot_ids = jnp.broadcast_to(jnp.arange(CAP, dtype=jnp.int32)[None, None, :], (devices, N_BLK, CAP))
    target_cells = donors.reshape(devices, N_BLK * CAP)[target_dev, sender_group * CAP + slot_ids]
    target_flat = (target_dev * ROWS + target_cells).reshape(-1)
    source_flat = (device_ids[:, None, None] * ROWS + sources).reshape(-1)
    sent = state[:, source_flat] * fringe_weight[None, :]
    image = image.at[:, target_flat].add(-sent)
    return image


def reference(residual_rhs, diag_blocks, jacobian_blocks, neighbors, partner, fringe_source, fringe_weight, fringe_donor, metric_sens, warp_row, warp_node, warp_weight):
    devices = N_BLK * N_SUB
    pivots = jnp.stack([diag_blocks[f, f] for f in range(FIELDS)]).astype(jnp.float32)
    state = relaxation * residual_rhs / pivots
    for sweep in range(SWEEPS):
        image = apply_operator(state, diag_blocks, jacobian_blocks, neighbors, partner, fringe_source, fringe_weight, fringe_donor)
        state = state + relaxation * (residual_rhs - image) / pivots
    volume = jnp.zeros((3, devices * ROWS), jnp.float32)
    for f in range(FIELDS):
        volume = volume + metric_sens[:, f].astype(jnp.float32) * state[f][None, :]
    owner_rows = jnp.repeat(jnp.arange(devices, dtype=jnp.int32) * ROWS, WARP_DEV) + warp_row
    terms = volume[:, owner_rows] * warp_weight[None, :]
    surface = jnp.zeros((3, NODES), jnp.float32).at[:, warp_node].add(terms)
    return state, surface
```

```python
import jax
import jax.numpy as jnp
from jax import lax
from jax.experimental import pallas as pl
from jax.experimental.pallas import tpu as pltpu
from jax.sharding import PartitionSpec as P

MESH = pl.DeviceIdType.MESH
F32, BF16, I32 = jnp.float32, jnp.bfloat16, jnp.int32

FIELDS = 6
NEIGH = 6
SWEEPS = 3
ROWS = 768
CHUNKS = 6
RIM = 256
LANES = 128
GZ = 8
GR = 8
SUBS = 4
DEVICES = 256
WARP_CHUNKS = 16
RELAX = 0.8


def split3(v):
    a = v.astype(BF16).astype(F32)
    b = (v - a).astype(BF16).astype(F32)
    return a, b, v - a - b


def lane_pick(sources, first, low, high):
    acc = jnp.zeros((8, LANES), F32)
    for n, src in enumerate(sources):
        got = jnp.take_along_axis(src, low, axis=1, mode="promise_in_bounds")
        acc = jnp.where(high == first + n, got, acc)
    return acc


def row8(ref, i, start=0):
    return jnp.broadcast_to(ref[i : i + 1, start : start + LANES], (8, LANES))


def dot_nt(a, b):
    return lax.dot_general(a, b, (((1,), (1,)), ((), ())), preferred_element_type=F32)


def kernel(
    rhs, diag, jac, nbr, partner, fsrc, fwei, fdon, metric, wrow, wnode, wwei,
    out_state, out_surf,
    states, coef, image, fsi, fwt, don1h, low1h, whi,
    send1, recv1_0, recv1_1, recv1_2, send2, recv2_0, recv2_1, recv2_2, rims,
    volume, spread, send_a, recv_a, send_b, recv_b,
    sem_s1, sem_r1, sem_s2, sem_r2, sem_sr, sem_rl, sem_ru, sem_fin,
):
    blk, sub = lax.axis_index("blk"), lax.axis_index("sub")
    y, z, core = blk // 16, (blk // 2) % GZ, blk % 2
    r = core * 4 + y
    dev = blk * SUBS + sub
    after, before = (dev + 1) % DEVICES, (dev + DEVICES - 1) % DEVICES

    def blk_of(zz, rr):
        return (rr % 4) * 16 + zz * 2 + rr // 4

    barrier = pltpu.get_barrier_semaphore()

    def greet(b, s):
        pl.semaphore_signal(barrier, inc=1, device_id=(b, s), device_id_type=MESH)

    for j in range(1, GZ):
        greet(blk_of((z + j) % GZ, r), sub)
    for j in range(1, GR * SUBS):
        greet(blk_of(z, (r + j // SUBS) % GR), (sub + j % SUBS) % SUBS)
    greet(after // SUBS, after % SUBS)
    greet(before // SUBS, before % SUBS)

    for n in range(SWEEPS + 1):
        states[n, FIELDS:8, :] = jnp.zeros((8 - FIELDS, ROWS), F32)
    for f in range(FIELDS):
        coef[f : f + 1, :] = RELAX / diag[f, f : f + 1, :].astype(F32)
    states[0, 0:FIELDS, :] = rhs[...] * coef[0:FIELDS, :]

    lane = lax.broadcasted_iota(I32, (8, LANES), 1)
    in_use = lane < 64
    for zz in range(GZ):
        pos = (zz * 16 + (lane >> 5) * 8 + (lane & 7)) & 127
        src = jnp.zeros((8, LANES), I32)
        wei = jnp.zeros((8, LANES), F32)
        for yy in range(4):
            mine = ((lane >> 3) & 3) == yy
            src = jnp.where(mine, jnp.take_along_axis(row8(fsrc, yy), pos, axis=1, mode="promise_in_bounds"), src)
            wei = jnp.where(mine, jnp.take_along_axis(row8(fwei, yy), pos, axis=1, mode="promise_in_bounds"), wei)
        fsi[zz] = jnp.where(in_use, src, 0)
        fwt[zz] = jnp.where(in_use, wei, 0.0)
    cell = lax.broadcasted_iota(I32, (512, LANES), 0)
    for rr in range(GR):
        pos = ((lane >> 3) * 16 + (rr // 4) * 8 + (lane & 7)) & 127
        don = jnp.take_along_axis(row8(fdon, rr % 4), pos, axis=1, mode="promise_in_bounds")
        don = jnp.where(in_use, don, -1)[0:1, :]
        don1h[:, rr * LANES : (rr + 1) * LANES] = jnp.where(cell == don, 1.0, 0.0).astype(BF16)
    spot = lax.broadcasted_iota(I32, (256, LANES), 0)
    for e in range(WARP_CHUNKS):
        node = wnode[e : e + 1, :]
        low1h[:, e * LANES : (e + 1) * LANES] = jnp.where(spot == (node & 255), 1.0, 0.0).astype(BF16)
    high = wnode[...] >> 8
    whi[...] = (high & 7) * 4 + (high >> 3)

    pl.semaphore_wait(barrier, (GZ - 1) + (GR * SUBS - 1) + 2)

    def send(src, dst, s_sem, r_sem, b, s):
        pltpu.make_async_remote_copy(
            src_ref=src, dst_ref=dst, send_sem=s_sem, recv_sem=r_sem, device_id=(b, s), device_id_type=MESH
        ).start()

    def drain(ref, sem):
        pltpu.make_async_copy(ref, ref, sem).wait()

    def sweep(n, recv1, recv2):
        send(states.at[n, :, pl.ds(256, 256)], rims.at[n, 0], sem_sr.at[n], sem_rl.at[n], after // SUBS, after % SUBS)
        send(states.at[n, :, pl.ds(0, 256)], rims.at[n, 1], sem_sr.at[n], sem_ru.at[n], before // SUBS, before % SUBS)
        own = [states[n, :, c * LANES : (c + 1) * LANES] for c in range(CHUNKS)]
        for j in range(GZ):
            zt = (z + j) % GZ
            idx = fsi[zt]
            out = lane_pick(own, 0, idx & 127, idx >> 7) * fwt[zt]
            if j == 0:
                recv1[z, :, 0:256] = states[n, :, 512:768]
                recv1[z, :, 256:384] = out
            else:
                send1[n, j - 1, :, 0:256] = states[n, :, 512:768]
                send1[n, j - 1, :, 256:384] = out
                send(send1.at[n, j - 1], recv1.at[z], sem_s1.at[n], sem_r1.at[n], blk_of(zt, r), sub)
        drain(send1.at[n], sem_r1.at[n])

        came = [recv1[zz, :, 256:384] for zz in range(GZ)]
        for rr in range(GR):
            out = jnp.zeros((8, LANES), F32)
            for zz in range(GZ):
                shift = ((zz - rr) * 8) % LANES
                moved = pltpu.roll(came[zz], shift, 1) if shift else came[zz]
                out = jnp.where((lane >> 3) == zz, moved, out)
            send2[n, rr, :, 256:384] = out
        for j in range(GR):
            rt = (r + j) % GR
            bt = blk_of(z, rt)
            block = recv1[(partner[bt] // 2) % GZ, :, 0:256]
            if j == 0:
                recv2[r, :, 0:256] = block
                recv2[r, :, 256:384] = send2[n, r, :, 256:384]
            else:
                send2[n, rt, :, 0:256] = block
                send(send2.at[n, rt], recv2.at[r], sem_s2.at[n], sem_r2.at[n], bt, sub)

        drain(rims.at[n, 0], sem_rl.at[n])
        drain(rims.at[n, 1], sem_ru.at[n])
        lower = [jnp.where(dev == 0, 0.0, rims[n, 0, :, c * LANES : (c + 1) * LANES]) for c in range(2)]
        upper = [jnp.where(dev == DEVICES - 1, 0.0, rims[n, 1, :, c * LANES : (c + 1) * LANES]) for c in range(2)]
        near = lower + own + upper

        def add_blocks(total, c, sources, first):
            at = slice(c * LANES, (c + 1) * LANES)
            for k in range(NEIGH):
                idx = row8(nbr, k, c * LANES)
                pick = lane_pick(sources, first, idx & 127, idx >> 7)
                for f in range(FIELDS):
                    total = total + jac[k, f, :, at].astype(F32) * pick[f : f + 1, :]
            return total

        for c in range(CHUNKS):
            at = slice(c * LANES, (c + 1) * LANES)
            total = jnp.zeros((FIELDS, LANES), F32)
            for f in range(FIELDS):
                total = total + diag[f, :, at].astype(F32) * own[c][f : f + 1, :]
            image[0:FIELDS, at] = add_blocks(total, c, near, 0)

        drain(send2.at[n, pl.ds(0, GR - 1)], sem_r2.at[n])
        mate = partner[blk]
        slot = (mate % 2) * 4 + mate // 16
        far = [recv2[slot, :, c * LANES : (c + 1) * LANES] for c in range(2)]
        arrived = jnp.concatenate([recv2[rr, :, 256:384] for rr in range(GR)], axis=1)
        parts = dot_nt(jnp.concatenate(split3(arrived), axis=0).astype(BF16), don1h[...])
        fringe = parts[0:8] + parts[8:16] + parts[16:24]
        for c in range(CHUNKS):
            at = slice(c * LANES, (c + 1) * LANES)
            total = add_blocks(image[0:FIELDS, at], c, far, 10)
            if c < 4:
                total = total - fringe[0:FIELDS, at]
            states[n + 1, 0:FIELDS, at] = own[c][0:FIELDS] + (rhs[:, at] - total) * coef[0:FIELDS, at]

    for n, hops in enumerate(((recv1_0, recv2_0), (recv1_1, recv2_1), (recv1_2, recv2_2))):
        sweep(n, *hops)

    final = states[SWEEPS, 0:FIELDS, :]
    out_state[...] = final
    volume[...] = jnp.zeros((8, ROWS), F32)
    for c in range(3):
        volume[c : c + 1, :] = jnp.sum(metric[c].astype(F32) * final, axis=0, keepdims=True)
    vol = [volume[:, c * LANES : (c + 1) * LANES] for c in range(CHUNKS)]
    hi_row = lax.broadcasted_iota(I32, (32, LANES), 0)
    for e in range(WARP_CHUNKS):
        at = slice(e * LANES, (e + 1) * LANES)
        idx = row8(wrow, e)
        terms = lane_pick(vol, 0, idx & 127, idx >> 7) * row8(wwei, e)
        here = hi_row == whi[e : e + 1, :]
        for p, part in enumerate(split3(terms)):
            for c in range(3):
                row = (p * 3 + c) * 32
                spread[row : row + 32, at] = jnp.where(here, part[c : c + 1, :], 0.0).astype(BF16)
    dense = dot_nt(spread[...], low1h[...])
    dense = dense[0:96] + dense[96:192] + dense[192:288]
    for zz in range(GZ):
        for c in range(3):
            row = c * 32 + zz * 4
            send_a[zz, c, 0:4, :] = dense[row : row + 4, 0:LANES]
            send_a[zz, c, 4:8, :] = dense[row : row + 4, LANES : 2 * LANES]
    recv_a[z] = send_a[z]
    for j in range(1, GZ):
        zt = (z + j) % GZ
        send(send_a.at[zt], recv_a.at[z], sem_fin.at[0], sem_fin.at[1], blk_of(zt, r), sub)
    drain(send_a.at[pl.ds(0, GZ - 1)], sem_fin.at[1])
    total = recv_a[0]
    for zz in range(1, GZ):
        total = total + recv_a[zz]
    for rr in range(GR):
        for c in range(3):
            send_b[rr, c : c + 1, :] = total[c, rr : rr + 1, :]
    recv_b[r * SUBS + sub] = send_b[r]
    for j in range(1, GR * SUBS):
        rt = (r + j // SUBS) % GR
        send(send_b.at[rt], recv_b.at[r * SUBS + sub], sem_fin.at[2], sem_fin.at[3], blk_of(z, rt), (sub + j % SUBS) % SUBS)
    drain(recv_b.at[pl.ds(0, GR * SUBS - 1)], sem_fin.at[3])
    surf = recv_b[0]
    for n in range(1, GR * SUBS):
        surf = surf + recv_b[n]
    out_surf[...] = surf

    for n in range(SWEEPS):
        drain(send1.at[n], sem_s1.at[n])
        drain(send2.at[n, pl.ds(0, GR - 1)], sem_s2.at[n])
        drain(rims.at[n], sem_sr.at[n])
    drain(send_a.at[pl.ds(0, GZ - 1)], sem_fin.at[0])
    drain(recv_b.at[pl.ds(0, GR * SUBS - 1)], sem_fin.at[2])


def body(
    residual_rhs, diag_blocks, jacobian_blocks, neighbors, partner, fringe_source, fringe_weight, fringe_donor,
    metric_sens, warp_row, warp_node, warp_weight,
):
    vmem = pl.BlockSpec(memory_space=pltpu.VMEM)
    smem = pl.BlockSpec(memory_space=pltpu.SMEM)
    v = pltpu.VMEM
    dma = pltpu.SemaphoreType.DMA
    return pl.pallas_call(
        kernel,
        out_shape=(
            jax.ShapeDtypeStruct((FIELDS, ROWS), F32),
            jax.ShapeDtypeStruct((3, LANES), F32),
        ),
        in_specs=[vmem] * 4 + [smem] + [vmem] * 7,
        out_specs=(vmem, vmem),
        scratch_shapes=[
            v((SWEEPS + 1, 8, ROWS), F32),
            v((8, ROWS), F32),
            v((8, ROWS), F32),
            v((GZ, 8, LANES), I32),
            v((GZ, 8, LANES), F32),
            v((512, GR * LANES), BF16),
            v((256, WARP_CHUNKS * LANES), BF16),
            v((WARP_CHUNKS, LANES), I32),
            v((SWEEPS, GZ - 1, 8, 384), F32),
            v((GZ, 8, 384), F32),
            v((GZ, 8, 384), F32),
            v((GZ, 8, 384), F32),
            v((SWEEPS, GR, 8, 384), F32),
            v((GR, 8, 384), F32),
            v((GR, 8, 384), F32),
            v((GR, 8, 384), F32),
            v((SWEEPS, 2, 8, RIM), F32),
            v((8, ROWS), F32),
            v((288, WARP_CHUNKS * LANES), BF16),
            v((GZ, 3, 8, LANES), F32),
            v((GZ, 3, 8, LANES), F32),
            v((GR, 3, LANES), F32),
            v((GR * SUBS, 3, LANES), F32),
        ]
        + [dma((SWEEPS,))] * 7
        + [dma((4,))],
        compiler_params=pltpu.CompilerParams(
            collective_id=0, has_side_effects=True, vmem_limit_bytes=40 * 1024 * 1024
        ),
    )(
        residual_rhs,
        diag_blocks,
        jacobian_blocks,
        neighbors,
        partner,
        fringe_source.reshape(4, LANES),
        fringe_weight.reshape(4, LANES),
        fringe_donor.reshape(4, LANES),
        metric_sens,
        warp_row.reshape(WARP_CHUNKS, LANES),
        warp_node.reshape(WARP_CHUNKS, LANES),
        warp_weight.reshape(WARP_CHUNKS, LANES),
    )


def solution(mesh):
    both = ("blk", "sub")
    in_specs = (
        P(None, both),
        P(None, None, both),
        P(None, None, None, both),
        P(None, both),
        P(),
        P(both),
        P(both),
        P(both),
        P(None, None, both),
        P(both),
        P(both),
        P(both),
    )
    out_specs = (P(None, both), P(None, "blk"))
    return jax.shard_map(body, mesh=mesh, in_specs=in_specs, out_specs=out_specs, check_vma=False)
```

```python
import jax
import jax.numpy as jnp
from jax import lax
from jax.experimental import pallas as pl
from jax.experimental.pallas import tpu as pltpu
from jax.sharding import PartitionSpec as P

MESH = pl.DeviceIdType.MESH
F32, BF16, I32 = jnp.float32, jnp.bfloat16, jnp.int32

FIELDS = 6
NEIGH = 6
SWEEPS = 3
ROWS = 768
CHUNKS = 6
RIM = 256
LANES = 128
GZ = 8
GR = 8
SUBS = 4
DEVICES = 256
WARP_CHUNKS = 16
RELAX = 0.8
FAR_FIRST = (4, 3, 5, 2, 6, 1, 7)


def split2(v):
    a = v.astype(BF16).astype(F32)
    return a, (v - a).astype(BF16).astype(F32)


def take(values, index):
    return jnp.take_along_axis(values, index, axis=1, mode="promise_in_bounds")


def lane_pick(sources, first, low, high, acc=None):
    acc = jnp.zeros((8, LANES), F32) if acc is None else acc
    for n, src in enumerate(sources):
        acc = jnp.where(high == first + n, take(src, low), acc)
    return acc


def row8(ref, i, start=0):
    return jnp.broadcast_to(ref[i : i + 1, start : start + LANES], (8, LANES))


def dot_nt(a, b):
    return lax.dot_general(a, b, (((1,), (1,)), ((), ())), preferred_element_type=F32)


def kernel(
    h_rhs, h_diag, h_jac, h_nbr, h_partner, h_fsrc, h_fwei, h_fdon, h_metric, h_wrow, h_wnode, h_wwei,
    out_state, out_surf,
    rhs, diag, jac, nbr, partner, fsrc, fwei, fdon, metric, wrow, wnode, wwei,
    states, coef, picks, blocks, fsi, fwt, don1h, low1h, whi,
    mates1_0, mates1_1, mates1_2, fwd, mates2_0, mates2_1, mates2_2,
    fsend1, frecv1, fsend2, frecv2, rims,
    volume, spread, send_a, recv_a, send_b, recv_b,
    sem_in, sem_m1s, sem_m1r, sem_m2s, sem_m2r, sem_f1s, sem_f1r, sem_f2s, sem_f2r, sem_sr, sem_rl, sem_ru, sem_fin,
):
    blk, sub = lax.axis_index("blk"), lax.axis_index("sub")
    y, z, core = blk // 16, (blk // 2) % GZ, blk % 2
    r = core * 4 + y
    dev = blk * SUBS + sub
    after, before = (dev + 1) % DEVICES, (dev + DEVICES - 1) % DEVICES
    mates1 = (mates1_0, mates1_1, mates1_2)
    mates2 = (mates2_0, mates2_1, mates2_2)

    def blk_of(zz, rr):
        return (rr % 4) * 16 + zz * 2 + rr // 4

    barrier = pltpu.get_barrier_semaphore()

    def greet(b, s):
        pl.semaphore_signal(barrier, inc=1, device_id=(b, s), device_id_type=MESH)

    for j in range(1, GZ):
        greet(blk_of((z + j) % GZ, r), sub)
    for j in range(1, GR * SUBS):
        greet(blk_of(z, (r + j // SUBS) % GR), (sub + j % SUBS) % SUBS)
    greet(after // SUBS, after % SUBS)
    greet(before // SUBS, before % SUBS)

    pairs = dict(
        rhs=(h_rhs, rhs), diag=(h_diag, diag), fsrc=(h_fsrc, fsrc), fwei=(h_fwei, fwei), partner=(h_partner, partner),
        jac=(h_jac, jac), nbr=(h_nbr, nbr), fdon=(h_fdon, fdon), wnode=(h_wnode, wnode), metric=(h_metric, metric),
        wrow=(h_wrow, wrow), wwei=(h_wwei, wwei),
    )
    fetch = {name: pltpu.make_async_copy(*pair, sem_in.at[n]) for n, (name, pair) in enumerate(pairs.items())}
    for copy in fetch.values():
        copy.start()

    for n in range(SWEEPS + 1):
        states[n, FIELDS:8, :] = jnp.zeros((8 - FIELDS, ROWS), F32)

    fetch["rhs"].wait()
    fetch["diag"].wait()
    for f in range(FIELDS):
        coef[f : f + 1, :] = RELAX / diag[f, f : f + 1, :].astype(F32)
    states[0, 0:FIELDS, :] = rhs[...] * coef[0:FIELDS, :]

    lane = lax.broadcasted_iota(I32, (8, LANES), 1)
    fetch["fsrc"].wait()
    fetch["fwei"].wait()
    for zz in range(GZ // 2):
        pos = zz * 32 + (lane >> 6) * 16 + ((lane >> 5) & 1) * 8 + (lane & 7)
        src = jnp.zeros((8, LANES), I32)
        wei = jnp.zeros((8, LANES), F32)
        for yy in range(4):
            mine = ((lane >> 3) & 3) == yy
            src = jnp.where(mine, take(row8(fsrc, yy), pos), src)
            wei = jnp.where(mine, take(row8(fwei, yy), pos), wei)
        fsi[zz] = src
        fwt[zz] = wei
    fetch["partner"].wait()
    fetch["nbr"].wait()
    fetch["jac"].wait()
    for k in range(NEIGH):
        for f in range(FIELDS):
            blocks[k * FIELDS + f, 0:FIELDS, :] = jac[k, f].astype(F32)

    pl.semaphore_wait(barrier, (GZ - 1) + (GR * SUBS - 1) + 2)

    def send(src, dst, s_sem, r_sem, b, s):
        pltpu.make_async_remote_copy(
            src_ref=src, dst_ref=dst, send_sem=s_sem, recv_sem=r_sem, device_id=(b, s), device_id_type=MESH
        ).start()

    def drain(ref, sem):
        pltpu.make_async_copy(ref, ref, sem).wait()

    def send_mates(n):
        for j in range(1, GZ):
            zt = (z + FAR_FIRST[j - 1]) % GZ
            send(states.at[n, :, pl.ds(512, 256)], mates1[n].at[z], sem_m1s.at[n], sem_m1r.at[n], blk_of(zt, r), sub)
        mates1[n][z] = states[n, :, 512:768]

    def send_cells(n):
        send(states.at[n, :, pl.ds(256, 256)], rims.at[n, 0], sem_sr.at[n], sem_rl.at[n], after // SUBS, after % SUBS)
        send(states.at[n, :, pl.ds(0, 256)], rims.at[n, 1], sem_sr.at[n], sem_ru.at[n], before // SUBS, before % SUBS)
        own = [states[n, :, c * LANES : (c + 1) * LANES] for c in range(CHUNKS)]
        for zz in range(GZ // 2):
            idx = fsi[zz]
            fsend1[n, zz] = lane_pick(own, 0, idx & 127, idx >> 7) * fwt[zz]
        for j in range(1, GZ):
            zt = (z + FAR_FIRST[j - 1]) % GZ
            send(fsend1.at[n, zt // 2], frecv1.at[n, z], sem_f1s.at[n], sem_f1r.at[n], blk_of(zt, r), sub)
        frecv1[n, z] = fsend1[n, z // 2]

    def pick_own(own):
        for c in range(CHUNKS):
            for k in range(NEIGH):
                idx = row8(nbr, k, c * LANES)
                picks[k, :, c * LANES : (c + 1) * LANES] = lane_pick(own, 2, idx & 127, idx >> 7)

    def pick_rims(lower, upper):
        for c in range(CHUNKS):
            at = slice(c * LANES, (c + 1) * LANES)
            for k in range(NEIGH):
                idx = row8(nbr, k, c * LANES)
                acc = lane_pick(lower, 0, idx & 127, idx >> 7, picks[k, :, at])
                picks[k, :, at] = lane_pick(upper, 8, idx & 127, idx >> 7, acc)

    def finish(n, c, far, fringe):
        at = slice(c * LANES, (c + 1) * LANES)
        sums = []
        for k in range(NEIGH):
            idx = row8(nbr, k, c * LANES)
            pick = lane_pick(far, 10, idx & 127, idx >> 7, picks[k, :, at])
            part = blocks[k * FIELDS, 0:FIELDS, at] * pick[0:1, :]
            for f in range(1, FIELDS):
                part = part + blocks[k * FIELDS + f, 0:FIELDS, at] * pick[f : f + 1, :]
            sums.append(part)
        old = states[n, :, at]
        part = diag[0, :, at].astype(F32) * old[0:1, :]
        for f in range(1, FIELDS):
            part = part + diag[f, :, at].astype(F32) * old[f : f + 1, :]
        total = (sums[0] + sums[1]) + (sums[2] + sums[3]) + (sums[4] + sums[5]) + part
        if fringe is not None:
            total = total - fringe[0:FIELDS, at]
        states[n + 1, 0:FIELDS, at] = old[0:FIELDS] + (rhs[:, at] - total) * coef[0:FIELDS, at]

    send_mates(0)
    send_cells(0)

    fetch["fdon"].wait()
    cell = lax.broadcasted_iota(I32, (512, LANES), 0)
    for rr in range(GR):
        pos = ((lane >> 3) * 16 + (rr // 4) * 8 + (lane & 7)) & 127
        don = jnp.where(lane < 64, take(row8(fdon, rr % 4), pos), -1)[0:1, :]
        don1h[:, rr * LANES : (rr + 1) * LANES] = jnp.where(cell == don, 1.0, 0.0).astype(BF16)
    fetch["wnode"].wait()
    spot = lax.broadcasted_iota(I32, (512, LANES), 0)
    for e in range(WARP_CHUNKS):
        node = wnode[e : e + 1, :]
        low1h[:, e * LANES : (e + 1) * LANES] = jnp.where(spot == (node & 511), 1.0, 0.0).astype(BF16)
    high = wnode[...] >> 9
    whi[...] = (high & 3) * 4 + (high >> 2)

    for n in range(SWEEPS):
        own = [states[n, :, c * LANES : (c + 1) * LANES] for c in range(CHUNKS)]
        pick_own(own)

        drain(mates1[n].at[pl.ds(0, GZ - 1)], sem_m1r.at[n])
        for j in range(GR):
            rt = (r + j) % GR
            bt = blk_of(z, rt)
            block = mates1[n][(partner[bt] // 2) % GZ]
            if j == 0:
                mates2[n][r] = block
            else:
                fwd[n, rt] = block
                send(fwd.at[n, rt], mates2[n].at[r], sem_m2s.at[n], sem_m2r.at[n], bt, sub)

        drain(frecv1.at[n, pl.ds(0, GZ - 1)], sem_f1r.at[n])
        odd = z % 2 == 1
        came = []
        for zz in range(GZ):
            v = frecv1[n, zz]
            came.append(jnp.where(odd, pltpu.roll(v, 64, 1), v))
        for rr in range(GR):
            out = jnp.zeros((8, LANES), F32)
            for zz in range(GZ):
                shift = ((zz - rr) * 8) % LANES
                moved = pltpu.roll(came[zz], shift, 1) if shift else came[zz]
                out = jnp.where((lane >> 3) == zz, moved, out)
            fsend2[n, rr] = out
        for j in range(1, GR):
            rt = (r + j) % GR
            send(fsend2.at[n, rt], frecv2.at[n, r], sem_f2s.at[n], sem_f2r.at[n], blk_of(z, rt), sub)
        frecv2[n, r] = fsend2[n, r]

        drain(rims.at[n, 0], sem_rl.at[n])
        drain(rims.at[n, 1], sem_ru.at[n])
        lower = [jnp.where(dev == 0, 0.0, rims[n, 0, :, c * LANES : (c + 1) * LANES]) for c in range(2)]
        upper = [jnp.where(dev == DEVICES - 1, 0.0, rims[n, 1, :, c * LANES : (c + 1) * LANES]) for c in range(2)]
        pick_rims(lower, upper)

        drain(mates2[n].at[pl.ds(0, GR - 1)], sem_m2r.at[n])
        mate = partner[blk]
        slot = (mate % 2) * 4 + mate // 16
        far = [mates2[n][slot, :, c * LANES : (c + 1) * LANES] for c in range(2)]
        for c in range(4, CHUNKS):
            finish(n, c, far, None)
        if n + 1 < SWEEPS:
            send_mates(n + 1)
        drain(frecv2.at[n, pl.ds(0, GR - 1)], sem_f2r.at[n])
        arrived = jnp.concatenate([frecv2[n, rr] for rr in range(GR)], axis=1)
        parts = dot_nt(jnp.concatenate(split2(arrived), axis=0).astype(BF16), don1h[...])
        fringe = parts[0:8] + parts[8:16]
        for c in range(4):
            finish(n, c, far, fringe)
        if n + 1 < SWEEPS:
            send_cells(n + 1)

    final = states[SWEEPS, 0:FIELDS, :]
    out_state[...] = final
    fetch["metric"].wait()
    fetch["wrow"].wait()
    fetch["wwei"].wait()
    volume[...] = jnp.zeros((8, ROWS), F32)
    for c in range(3):
        volume[c : c + 1, :] = jnp.sum(metric[c].astype(F32) * final, axis=0, keepdims=True)
    vol = [volume[:, c * LANES : (c + 1) * LANES] for c in range(CHUNKS)]
    hi_row = lax.broadcasted_iota(I32, (16, LANES), 0)
    for e in range(WARP_CHUNKS):
        at = slice(e * LANES, (e + 1) * LANES)
        idx = row8(wrow, e)
        terms = lane_pick(vol, 0, idx & 127, idx >> 7) * row8(wwei, e)
        here = hi_row == whi[e : e + 1, :]
        for p, part in enumerate(split2(terms)):
            for c in range(3):
                row = (p * 3 + c) * 16
                spread[row : row + 16, at] = jnp.where(here, part[c : c + 1, :], 0.0).astype(BF16)
    dense = dot_nt(spread[...], low1h[...])
    dense = dense[0:48] + dense[48:96]
    for zz in range(GZ):
        for c in range(3):
            row = c * 16 + (zz // 2) * 4
            col = (zz % 2) * 256
            send_a[zz, c, 0:4, :] = dense[row : row + 4, col : col + LANES]
            send_a[zz, c, 4:8, :] = dense[row : row + 4, col + LANES : col + 2 * LANES]
    for j in range(1, GZ):
        zt = (z + FAR_FIRST[j - 1]) % GZ
        send(send_a.at[zt], recv_a.at[z], sem_fin.at[0], sem_fin.at[1], blk_of(zt, r), sub)
    recv_a[z] = send_a[z]
    drain(send_a.at[pl.ds(0, GZ - 1)], sem_fin.at[1])
    total = recv_a[0]
    for zz in range(1, GZ):
        total = total + recv_a[zz]
    for rr in range(GR):
        for c in range(3):
            send_b[rr, c : c + 1, :] = total[c, rr : rr + 1, :]
    for j in range(1, GR * SUBS):
        rt = (r + j // SUBS) % GR
        send(send_b.at[rt], recv_b.at[r * SUBS + sub], sem_fin.at[2], sem_fin.at[3], blk_of(z, rt), (sub + j % SUBS) % SUBS)
    recv_b[r * SUBS + sub] = send_b[r]
    drain(recv_b.at[pl.ds(0, GR * SUBS - 1)], sem_fin.at[3])
    surf = recv_b[0]
    for n in range(1, GR * SUBS):
        surf = surf + recv_b[n]
    out_surf[...] = surf

    for n in range(SWEEPS):
        drain(mates1[n].at[pl.ds(0, GZ - 1)], sem_m1s.at[n])
        drain(fwd.at[n, pl.ds(0, GR - 1)], sem_m2s.at[n])
        drain(frecv1.at[n, pl.ds(0, GZ - 1)], sem_f1s.at[n])
        drain(fsend2.at[n, pl.ds(0, GR - 1)], sem_f2s.at[n])
        drain(rims.at[n], sem_sr.at[n])
    drain(send_a.at[pl.ds(0, GZ - 1)], sem_fin.at[0])
    drain(recv_b.at[pl.ds(0, GR * SUBS - 1)], sem_fin.at[2])


def body(
    residual_rhs, diag_blocks, jacobian_blocks, neighbors, partner, fringe_source, fringe_weight, fringe_donor,
    metric_sens, warp_row, warp_node, warp_weight,
):
    vmem = pl.BlockSpec(memory_space=pltpu.VMEM)
    hbm = pl.BlockSpec(memory_space=pltpu.HBM)
    v = pltpu.VMEM
    dma = pltpu.SemaphoreType.DMA
    operands = (
        residual_rhs,
        diag_blocks,
        jacobian_blocks,
        neighbors,
        partner,
        fringe_source.reshape(4, LANES),
        fringe_weight.reshape(4, LANES),
        fringe_donor.reshape(4, LANES),
        metric_sens,
        warp_row.reshape(WARP_CHUNKS, LANES),
        warp_node.reshape(WARP_CHUNKS, LANES),
        warp_weight.reshape(WARP_CHUNKS, LANES),
    )
    return pl.pallas_call(
        kernel,
        out_shape=(
            jax.ShapeDtypeStruct((FIELDS, ROWS), F32),
            jax.ShapeDtypeStruct((3, LANES), F32),
        ),
        in_specs=[hbm] * 12,
        out_specs=(vmem, vmem),
        scratch_shapes=[(pltpu.SMEM if n == 4 else v)(o.shape, o.dtype) for n, o in enumerate(operands)]
        + [
            v((SWEEPS + 1, 8, ROWS), F32),
            v((8, ROWS), F32),
            v((NEIGH, 8, ROWS), F32),
            v((NEIGH * FIELDS, 8, ROWS), F32),
            v((GZ // 2, 8, LANES), I32),
            v((GZ // 2, 8, LANES), F32),
            v((512, GR * LANES), BF16),
            v((512, WARP_CHUNKS * LANES), BF16),
            v((WARP_CHUNKS, LANES), I32),
        ]
        + [v((GZ, 8, 256), F32)] * SWEEPS
        + [v((SWEEPS, GR, 8, 256), F32)]
        + [v((GR, 8, 256), F32)] * SWEEPS
        + [
            v((SWEEPS, GZ // 2, 8, LANES), F32),
            v((SWEEPS, GZ, 8, LANES), F32),
            v((SWEEPS, GR, 8, LANES), F32),
            v((SWEEPS, GR, 8, LANES), F32),
            v((SWEEPS, 2, 8, RIM), F32),
            v((8, ROWS), F32),
            v((96, WARP_CHUNKS * LANES), BF16),
            v((GZ, 3, 8, LANES), F32),
            v((GZ, 3, 8, LANES), F32),
            v((GR, 3, LANES), F32),
            v((GR * SUBS, 3, LANES), F32),
        ]
        + [dma((12,))]
        + [dma((SWEEPS,))] * 11
        + [dma((4,))],
        compiler_params=pltpu.CompilerParams(
            collective_id=0, has_side_effects=True, vmem_limit_bytes=60 * 1024 * 1024
        ),
    )(*operands)


def solution(mesh):
    both = ("blk", "sub")
    in_specs = (
        P(None, both),
        P(None, None, both),
        P(None, None, None, both),
        P(None, both),
        P(),
        P(both),
        P(both),
        P(both),
        P(None, None, both),
        P(both),
        P(both),
        P(both),
    )
    out_specs = (P(None, both), P(None, "blk"))
    return jax.shard_map(body, mesh=mesh, in_specs=in_specs, out_specs=out_specs, check_vma=False)
```
